32 devices in a mesh: samp: 16 (over z, y, x), trait: 2 (over core).
Axes of the slice: x: 2, y: 2, z: 4, core: 2. Of those that a mesh axis runs over, the one named last changes fastest.
Arguments:
- samples: bfloat16 [8192, 2048], P('samp'), may hold values from -18 to 18
- traits: bfloat16 [8192, 2048], P('samp', 'trait'), may hold values from -6 to 6
- whitening: bfloat16 [2048, 2048], P(None, 'trait'), may hold values from -0.0017089844 to 0.0017089844
- singular: float32 [2048], replicated, may hold values from 0.3 to 3
- lambdas: float32 [4], replicated, may hold values from 0.1 to 10
Outputs:
- loo_residual: float32 [4, 8192, 2048], P(None, 'samp', 'trait')
The draws below stay inside these ranges and needn't reach their ends.
All inputs are finite; a program needn't handle non-finite values.
Results may differ from the reference program's by a relative error of at most 0.0041.
Values may be sent and summed in bfloat16 or wider, within the bound.
A program may use at most 64 MiB of HBM per device.

```python
import math
import jax
import jax.numpy as jnp
from jax import lax

P_SIZE = 2048
T_SIZE = 2048
NL = 4
SAMPLES = 8192


def draw_samples(key, part):
    first_key, second_key = jax.random.split(jax.random.fold_in(key, 11), 2)
    row_scale = jnp.exp(jax.random.uniform(first_key, (SAMPLES, 1), jnp.float32, jnp.log(0.3), jnp.log(3.0)))
    base_values = jnp.clip(jax.random.normal(second_key, (SAMPLES, P_SIZE), jnp.float32), -6.0, 6.0)
    return (base_values * row_scale).astype(jnp.bfloat16)


def block_levels(stream_key, dims, cuts, low, top_value):
    def one(axis_at, shards_of):
        draws = jax.random.uniform(jax.random.fold_in(jax.random.fold_in(stream_key, 6), axis_at), (shards_of,), jnp.float32, low / len(cuts), top_value / len(cuts))
        return jnp.repeat(jnp.exp(draws), dims[axis_at] // shards_of).reshape((-1,) + (1,) * (len(dims) - axis_at - 1))

    gain = one(*cuts[0])
    for cut in cuts[1:]:
        gain = gain * one(*cut)
    return gain


def normal_values(stream_key, shape, scale, reach, cuts=(), kind=jnp.bfloat16):
    array = scale * jax.random.normal(stream_key, shape, jnp.float32)
    if cuts:
        array = array * block_levels(stream_key, shape, cuts, -0.22, 0.18)
    return jnp.clip(array, -reach, reach).astype(kind)


def setup_inputs(seed: int = 0) -> dict:
    seeds = jax.random.split(jax.random.key(seed), 6)
    samples = draw_samples(jax.random.fold_in(seeds[5], 71), 0)
    traits = normal_values(seeds[1], (SAMPLES, T_SIZE), 1.0, 6.0, ((0, 16), (1, 2)))
    whitening = normal_values(seeds[2], (P_SIZE, P_SIZE), (10 * P_SIZE * P_SIZE // 3) ** -0.5, 0.0017089844, ((1, 2),))
    singular = jnp.clip(jnp.exp(jax.random.uniform(seeds[3], (P_SIZE,), jnp.float32, math.log(0.3), math.log(3.0))), 0.3, 3.0)
    lambdas = jnp.clip(jnp.exp(jax.random.uniform(seeds[4], (NL,), jnp.float32, math.log(0.1), math.log(10.0))), 0.1, 10.0)
    return {"samples": samples, "traits": traits, "whitening": whitening, "singular": singular, "lambdas": lambdas}


def reference(samples, traits, whitening, singular, lambdas):
    components = jnp.dot(samples, whitening, preferred_element_type=jnp.float32).astype(jnp.bfloat16)
    squared_values = singular * singular
    shrink = squared_values[:, None] / (squared_values[:, None] + lambdas[None, :])
    wide_float = components.astype(jnp.float32)
    leverage = jnp.dot(wide_float * wide_float, shrink, precision=lax.Precision.HIGHEST)
    projected = jnp.dot(components.T, traits, preferred_element_type=jnp.float32).astype(jnp.bfloat16)
    target = traits.astype(jnp.float32)
    results = []
    for penalty in range(NL):
        scaled = (shrink[:, penalty:penalty + 1] * projected.astype(jnp.float32)).astype(jnp.bfloat16)
        fitted = jnp.dot(components, scaled, preferred_element_type=jnp.float32)
        divisor = jnp.maximum(1.0 - leverage[:, penalty:penalty + 1], 0.25)
        results.append((target - fitted) / divisor)
    return jnp.stack(results, axis=0)
```

```python
import functools

import jax
import jax.numpy as jnp
from jax import lax
from jax.experimental import pallas as pl
from jax.experimental.pallas import tpu as pltpu
from jax.sharding import PartitionSpec as P

MESH = pl.DeviceIdType.MESH
F32 = jnp.float32
BF16 = jnp.bfloat16
LANES = 128
ROWS = 16


def bit_orders(bits):
    rest = list(range(bits))
    if bits < 3:
        return [rest, rest[::-1]]
    a, b = rest, [1, 0] + rest[2:]
    c, d = [2, 0, 1] + rest[3:], [2, 1, 0] + rest[3:]
    return [a, b, c, a, b, d, a, b]


def exchange_kernel(
    n, nt, nl,
    s_ref, w_ref, y_ref, sing_ref, lam_ref,
    c_ref, pj_ref, lev_ref, shr_ref,
    acc, pb, rb, rs_send, rs_recv, ag_send, ag_recv, c_send, c_recv,
):
    bits = n.bit_length() - 1
    units, unit, _ = acc.shape
    own_k = c_ref.shape[2]
    own = own_k // unit
    orders = bit_orders(bits)
    me, mt = lax.axis_index("samp"), lax.axis_index("trait")
    value = [lax.rem(lax.div(me, 1 << b), 2) for b in range(bits)]
    peer = [me + (1 - 2 * value[b]) * (1 << b) for b in range(bits)]
    others = [lax.rem(mt + d, nt) for d in range(1, nt)]

    barrier = pltpu.get_barrier_semaphore()
    for p in peer:
        pl.semaphore_signal(barrier, inc=1, device_id=(p, mt), device_id_type=MESH)
    for t in others:
        pl.semaphore_signal(barrier, inc=1, device_id=(me, t), device_id_type=MESH)

    def rows(start, size):
        return pl.ds(pl.multiple_of(start, ROWS), size)

    def order(s):
        return orders[s % len(orders)]

    keep, give = [], []
    for s in range(units):
        start, keeps, gives = 0, [], []
        for j, b in enumerate(order(s)):
            size = unit >> (j + 1)
            keeps.append(start + value[b] * size)
            gives.append(start + (1 - value[b]) * size)
            start = keeps[-1]
        keep.append(keeps)
        give.append(gives)

    def place(s):
        if own:
            return lax.rem(mt + s // own, nt) * own + s % own
        return s

    def rs_copy(s, j):
        size = unit >> (j + 1)
        return pltpu.make_async_remote_copy(
            src_ref=pb.at[s, rows(give[s][j], size)],
            dst_ref=rb.at[s, pl.ds(unit - (unit >> j), size)],
            send_sem=rs_send.at[s, j],
            recv_sem=rs_recv.at[s, j],
            device_id=(peer[order(s)[j]], mt),
            device_id_type=MESH,
        )

    def ag_copy(s, j):
        size = unit >> (j + 1)
        held = pj_ref.at[place(s), rows(keep[s][j], size)]
        return pltpu.make_async_remote_copy(
            src_ref=held,
            dst_ref=held,
            send_sem=ag_send.at[s, j],
            recv_sem=ag_recv.at[s, j],
            device_id=(peer[order(s)[j]], mt),
            device_id_type=MESH,
        )

    def c_copy(d):
        return pltpu.make_async_remote_copy(
            src_ref=c_ref.at[mt],
            dst_ref=c_ref.at[mt],
            send_sem=c_send.at[d],
            recv_sem=c_recv.at[d],
            device_id=(me, others[d]),
            device_id_type=MESH,
        )

    contract_rows = (((0,), (0,)), ((), ()))

    def project(s):
        if own:
            t = lax.rem(mt + s // own, nt)
            part = c_ref[t, :, (s % own) * unit:(s % own + 1) * unit]
            acc[s] = lax.dot_general(part, y_ref[...], contract_rows, preferred_element_type=F32)
        else:
            pieces = unit // own_k
            for i in range(pieces):
                acc[s, i * own_k:(i + 1) * own_k, :] = lax.dot_general(
                    c_ref[s * pieces + i], y_ref[...], contract_rows, preferred_element_type=F32
                )
        size = unit >> 1
        pb[s, rows(give[s][0], size), :] = acc[s, rows(give[s][0], size), :].astype(BF16)

    block = min(unit, own_k)
    for q in range(own_k // block):
        cols = slice(q * block, (q + 1) * block)
        c_ref[mt, :, cols] = jnp.dot(
            s_ref[...], w_ref[:, cols], preferred_element_type=F32
        ).astype(BF16)
        if own:
            project(q)
        if q == 0:
            pl.semaphore_wait(barrier, bits + nt - 1)
        if own:
            rs_copy(q, 0).start()
    for d in range(nt - 1):
        c_copy(d).start()
    for d in range(nt - 1):
        c_copy(d).wait_recv()
    for s in range(own, units):
        project(s)
        rs_copy(s, 0).start()

    for j in range(bits):
        size = unit >> (j + 1)
        base = unit - (unit >> j)
        for s in range(units):
            rs_copy(s, j).wait_recv()
            if j + 1 < bits:
                half = size >> 1
                first = give[s][j + 1]
                landed = rb[s, rows(base + first - keep[s][j], half), :].astype(F32)
                pb[s, rows(first, half), :] = (acc[s, rows(first, half), :] + landed).astype(BF16)
                rs_copy(s, j + 1).start()
                second = keep[s][j + 1]
                landed = rb[s, rows(base + second - keep[s][j], half), :].astype(F32)
                acc[s, rows(second, half), :] = acc[s, rows(second, half), :] + landed
            else:
                total = acc[s, rows(keep[s][j], size), :] + rb[s, base:base + size, :].astype(F32)
                pj_ref[place(s), rows(keep[s][j], size), :] = total.astype(BF16)
                ag_copy(s, j).start()

    for j in range(bits - 2, -1, -1):
        for s in range(units):
            ag_copy(s, j + 1).wait_recv()
            ag_copy(s, j).start()

    squared = sing_ref[...] * sing_ref[...]
    row = lax.broadcasted_iota(jnp.int32, (LANES, squared.shape[1]), 0)
    lam = jnp.full(row.shape, 1.0, F32)
    for l in range(nl):
        lam = jnp.where(row == l, lam_ref[l], lam)
    shrink = squared / (squared + lam)
    shr_ref[...] = shrink.T
    tall = c_ref.shape[1]
    step = min(64, tall)

    @pl.loop(0, tall // step)
    def _(i):
        here = pl.ds(pl.multiple_of(i * step, step), step)
        sums = [jnp.zeros((step, 1), F32) for _ in range(nl)]
        for t in range(nt):
            wide = c_ref[t, here, :].astype(F32)
            wide = wide * wide
            for l in range(nl):
                weight = shrink[l:l + 1, t * own_k:(t + 1) * own_k]
                sums[l] = sums[l] + jnp.sum(wide * weight, axis=1, keepdims=True)
        lane = lax.broadcasted_iota(jnp.int32, (step, LANES), 1)
        result = jnp.zeros((step, LANES), F32)
        for l in range(nl):
            result = jnp.where(lane == l, sums[l], result)
        lev_ref[here, :] = result

    for s in range(units):
        ag_copy(s, 0).wait_recv()
    for d in range(nt - 1):
        c_copy(d).wait_send()
    for s in range(units):
        for j in range(bits):
            rs_copy(s, j).wait_send()
            ag_copy(s, j).wait_send()


def fit_kernel(nl, nt, c_ref, pj_ref, shr_ref, lev_ref, y_ref, out_ref):
    own_k = c_ref.shape[2]
    target = y_ref[...].astype(F32)
    for l in range(nl):
        fitted = jnp.zeros(target.shape, F32)
        for t in range(nt):
            here = slice(t * own_k, (t + 1) * own_k)
            wide = pj_ref[here, :].astype(F32)
            scaled = (shr_ref[here, l:l + 1] * wide).astype(BF16)
            fitted = fitted + jnp.dot(c_ref[t], scaled, preferred_element_type=F32)
        divisor = jnp.maximum(1.0 - lev_ref[:, l:l + 1], 0.25)
        out_ref[l] = (target - fitted) * (1.0 / divisor)


def local(n, nt, samples, traits, whitening, singular, lambdas):
    tall, k = samples.shape
    own_k = whitening.shape[1]
    wide = traits.shape[1]
    nl = lambdas.shape[0]
    bits = n.bit_length() - 1
    unit = ROWS << bits
    units = k // unit
    vmem = pl.BlockSpec(memory_space=pltpu.VMEM)
    components, projected, leverage, shrink = pl.pallas_call(
        functools.partial(exchange_kernel, n, nt, nl),
        out_shape=[
            jax.ShapeDtypeStruct((nt, tall, own_k), BF16),
            jax.ShapeDtypeStruct((units, unit, wide), BF16),
            jax.ShapeDtypeStruct((tall, LANES), F32),
            jax.ShapeDtypeStruct((k, LANES), F32),
        ],
        in_specs=[vmem] * 4 + [pl.BlockSpec(memory_space=pltpu.SMEM)],
        out_specs=[vmem] * 4,
        scratch_shapes=[
            pltpu.VMEM((units, unit, wide), F32),
            pltpu.VMEM((units, unit, wide), BF16),
            pltpu.VMEM((units, unit, wide), BF16),
            pltpu.SemaphoreType.DMA((units, bits)),
            pltpu.SemaphoreType.DMA((units, bits)),
            pltpu.SemaphoreType.DMA((units, bits)),
            pltpu.SemaphoreType.DMA((units, bits)),
            pltpu.SemaphoreType.DMA((nt - 1,)),
            pltpu.SemaphoreType.DMA((nt - 1,)),
        ],
        compiler_params=pltpu.CompilerParams(
            collective_id=0, has_side_effects=True, vmem_limit_bytes=56 * 2**20
        ),
        name="project_and_sum",
    )(samples, whitening, traits, singular.reshape(1, k), lambdas)
    projected = projected.reshape(k, wide)
    tile = min(256, wide)
    return pl.pallas_call(
        functools.partial(fit_kernel, nl, nt),
        grid=(wide // tile,),
        out_shape=jax.ShapeDtypeStruct((nl, tall, wide), F32),
        in_specs=[
            pl.BlockSpec((nt, tall, own_k), lambda i: (0, 0, 0)),
            pl.BlockSpec((k, tile), lambda i: (0, i)),
            pl.BlockSpec((k, LANES), lambda i: (0, 0)),
            pl.BlockSpec((tall, LANES), lambda i: (0, 0)),
            pl.BlockSpec((tall, tile), lambda i: (0, i)),
        ],
        out_specs=pl.BlockSpec((nl, tall, tile), lambda i: (0, 0, i)),
        compiler_params=pltpu.CompilerParams(vmem_limit_bytes=48 * 2**20),
        name="fit",
    )(components, projected, shrink, leverage, traits)


def solution(mesh):
    n, nt = mesh.shape["samp"], mesh.shape["trait"]
    return jax.shard_map(
        functools.partial(local, n, nt),
        mesh=mesh,
        in_specs=(P("samp", None), P("samp", "trait"), P(None, "trait"), P(), P()),
        out_specs=P(None, "samp", "trait"),
        check_vma=False,
    )
```

```python
import functools

import jax
import jax.numpy as jnp
from jax import lax
from jax.experimental import pallas as pl
from jax.experimental.pallas import tpu as pltpu
from jax.sharding import PartitionSpec as P

MESH = pl.DeviceIdType.MESH
F32 = jnp.float32
BF16 = jnp.bfloat16
LANES = 128
ROWS = 16


WAVE = 3


def bit_orders(bits):
    rest = list(range(bits))
    if bits < 3:
        return [rest, rest[::-1]]
    a, b, c = [0, 1, 2] + rest[3:], [1, 2, 0] + rest[3:], [2, 0, 1] + rest[3:]
    return [a, b, c, a, b, c, a, [1, 0, 2] + rest[3:]]


def exchange_kernel(
    n, nt, nl,
    s_ref, w_ref, y_ref, sing_ref, lam_ref,
    c_ref, pj_ref, lev_ref, shr_ref,
    acc, pb, rb, rs_send, rs_recv, ag_send, ag_recv, c_send, c_recv,
):
    bits = n.bit_length() - 1
    units, unit, _ = acc.shape
    own_k = c_ref.shape[2]
    own = own_k // unit
    orders = bit_orders(bits)
    me, mt = lax.axis_index("samp"), lax.axis_index("trait")
    value = [lax.rem(lax.div(me, 1 << b), 2) for b in range(bits)]
    peer = [me + (1 - 2 * value[b]) * (1 << b) for b in range(bits)]
    others = [lax.rem(mt + d, nt) for d in range(1, nt)]

    barrier = pltpu.get_barrier_semaphore()
    for p in peer:
        pl.semaphore_signal(barrier, inc=1, device_id=(p, mt), device_id_type=MESH)
    for t in others:
        pl.semaphore_signal(barrier, inc=1, device_id=(me, t), device_id_type=MESH)

    def rows(start, size):
        return pl.ds(pl.multiple_of(start, ROWS), size)

    def order(s):
        return orders[s % len(orders)]

    keep, give = [], []
    for s in range(units):
        start, keeps, gives = 0, [], []
        for j, b in enumerate(order(s)):
            size = unit >> (j + 1)
            keeps.append(start + value[b] * size)
            gives.append(start + (1 - value[b]) * size)
            start = keeps[-1]
        keep.append(keeps)
        give.append(gives)

    def place(s):
        if own:
            return lax.rem(mt + s // own, nt) * own + s % own
        return s

    def rs_copy(s, j):
        size = unit >> (j + 1)
        return pltpu.make_async_remote_copy(
            src_ref=pb.at[s, rows(give[s][j], size)],
            dst_ref=rb.at[s, pl.ds(unit - (unit >> j), size)],
            send_sem=rs_send.at[s, j],
            recv_sem=rs_recv.at[s, j],
            device_id=(peer[order(s)[j]], mt),
            device_id_type=MESH,
        )

    def ag_copy(s, j):
        size = unit >> (j + 1)
        held = pj_ref.at[place(s), rows(keep[s][j], size)]
        return pltpu.make_async_remote_copy(
            src_ref=held,
            dst_ref=held,
            send_sem=ag_send.at[s, j],
            recv_sem=ag_recv.at[s, j],
            device_id=(peer[order(s)[j]], mt),
            device_id_type=MESH,
        )

    def c_copy(d):
        return pltpu.make_async_remote_copy(
            src_ref=c_ref.at[mt],
            dst_ref=c_ref.at[mt],
            send_sem=c_send.at[d],
            recv_sem=c_recv.at[d],
            device_id=(me, others[d]),
            device_id_type=MESH,
        )

    contract_rows = (((0,), (0,)), ((), ()))

    def project(s):
        if own:
            t = lax.rem(mt + s // own, nt)
            part = c_ref[t, :, (s % own) * unit:(s % own + 1) * unit]
            acc[s] = lax.dot_general(part, y_ref[...], contract_rows, preferred_element_type=F32)
        else:
            pieces = unit // own_k
            for i in range(pieces):
                acc[s, i * own_k:(i + 1) * own_k, :] = lax.dot_general(
                    c_ref[s * pieces + i], y_ref[...], contract_rows, preferred_element_type=F32
                )
        size = unit >> 1
        pb[s, rows(give[s][0], size), :] = acc[s, rows(give[s][0], size), :].astype(BF16)

    block = min(unit, own_k)

    def own_block(q):
        cols = slice(q * block, (q + 1) * block)
        c_ref[mt, :, cols] = jnp.dot(
            s_ref[...], w_ref[:, cols], preferred_element_type=F32
        ).astype(BF16)
        if q == own_k // block - 1:
            if q == 0:
                pl.semaphore_wait(barrier, bits + nt - 1)
            for d in range(nt - 1):
                c_copy(d).start()

    def begin(s):
        if own:
            if s < own:
                own_block(s)
            if s == own:
                for d in range(nt - 1):
                    c_copy(d).wait_recv()
        elif s == 0:
            for q in range(own_k // block):
                own_block(q)
            for d in range(nt - 1):
                c_copy(d).wait_recv()
        project(s)
        if s == 0 and own_k > block:
            pl.semaphore_wait(barrier, bits + nt - 1)
        rs_copy(s, 0).start()

    def halve(s, j):
        size = unit >> (j + 1)
        base = unit - (unit >> j)
        rs_copy(s, j).wait_recv()
        if j + 1 < bits:
            half = size >> 1
            first = give[s][j + 1]
            landed = rb[s, rows(base + first - keep[s][j], half), :].astype(F32)
            pb[s, rows(first, half), :] = (acc[s, rows(first, half), :] + landed).astype(BF16)
            rs_copy(s, j + 1).start()
            second = keep[s][j + 1]
            landed = rb[s, rows(base + second - keep[s][j], half), :].astype(F32)
            acc[s, rows(second, half), :] = acc[s, rows(second, half), :] + landed
        else:
            total = acc[s, rows(keep[s][j], size), :] + rb[s, base:base + size, :].astype(F32)
            pj_ref[place(s), rows(keep[s][j], size), :] = total.astype(BF16)
            ag_copy(s, j).start()

    def double(s, j):
        ag_copy(s, j).wait_recv()
        if j > 0:
            ag_copy(s, j - 1).start()

    def leverage():
        squared = sing_ref[...] * sing_ref[...]
        row = lax.broadcasted_iota(jnp.int32, (LANES, squared.shape[1]), 0)
        lam = jnp.full(row.shape, 1.0, F32)
        for l in range(nl):
            lam = jnp.where(row == l, lam_ref[l], lam)
        shrink = squared / (squared + lam)
        shr_ref[...] = shrink.T
        tall = c_ref.shape[1]
        step = min(64, tall)

        @pl.loop(0, tall // step)
        def _(i):
            here = pl.ds(pl.multiple_of(i * step, step), step)
            sums = [jnp.zeros((step, 1), F32) for _ in range(nl)]
            for t in range(nt):
                wide = c_ref[t, here, :].astype(F32)
                wide = wide * wide
                for l in range(nl):
                    weight = shrink[l:l + 1, t * own_k:(t + 1) * own_k]
                    sums[l] = sums[l] + jnp.sum(wide * weight, axis=1, keepdims=True)
            lane = lax.broadcasted_iota(jnp.int32, (step, LANES), 1)
            result = jnp.zeros((step, LANES), F32)
            for l in range(nl):
                result = jnp.where(lane == l, sums[l], result)
            lev_ref[here, :] = result

    waves = [range(s, min(s + WAVE, units)) for s in range(0, units, WAVE)]
    for k in range(2 * bits + len(waves)):
        for w, wave in enumerate(waves):
            for s in wave:
                stage = k - w
                if stage == 0:
                    begin(s)
                elif 0 < stage <= bits:
                    halve(s, stage - 1)
                elif bits < stage <= 2 * bits:
                    double(s, 2 * bits - stage)
        if k == 2 * bits - 1:
            leverage()

    for d in range(nt - 1):
        c_copy(d).wait_send()
    for s in range(units):
        for j in range(bits):
            rs_copy(s, j).wait_send()
            ag_copy(s, j).wait_send()


def fit_kernel(nl, nt, c_ref, pj_ref, shr_ref, lev_ref, y_ref, out_ref):
    own_k = c_ref.shape[2]
    target = y_ref[...].astype(F32)
    for l in range(nl):
        fitted = jnp.zeros(target.shape, F32)
        for t in range(nt):
            here = slice(t * own_k, (t + 1) * own_k)
            wide = pj_ref[here, :].astype(F32)
            scaled = (shr_ref[here, l:l + 1] * wide).astype(BF16)
            fitted = fitted + jnp.dot(c_ref[t], scaled, preferred_element_type=F32)
        divisor = jnp.maximum(1.0 - lev_ref[:, l:l + 1], 0.25)
        out_ref[l] = (target - fitted) * (1.0 / divisor)


def local(n, nt, samples, traits, whitening, singular, lambdas):
    tall, k = samples.shape
    own_k = whitening.shape[1]
    wide = traits.shape[1]
    nl = lambdas.shape[0]
    bits = n.bit_length() - 1
    unit = ROWS << bits
    units = k // unit
    vmem = pl.BlockSpec(memory_space=pltpu.VMEM)
    components, projected, leverage, shrink = pl.pallas_call(
        functools.partial(exchange_kernel, n, nt, nl),
        out_shape=[
            jax.ShapeDtypeStruct((nt, tall, own_k), BF16),
            jax.ShapeDtypeStruct((units, unit, wide), BF16),
            jax.ShapeDtypeStruct((tall, LANES), F32),
            jax.ShapeDtypeStruct((k, LANES), F32),
        ],
        in_specs=[vmem] * 4 + [pl.BlockSpec(memory_space=pltpu.SMEM)],
        out_specs=[vmem] * 4,
        scratch_shapes=[
            pltpu.VMEM((units, unit, wide), F32),
            pltpu.VMEM((units, unit, wide), BF16),
            pltpu.VMEM((units, unit, wide), BF16),
            pltpu.SemaphoreType.DMA((units, bits)),
            pltpu.SemaphoreType.DMA((units, bits)),
            pltpu.SemaphoreType.DMA((units, bits)),
            pltpu.SemaphoreType.DMA((units, bits)),
            pltpu.SemaphoreType.DMA((nt - 1,)),
            pltpu.SemaphoreType.DMA((nt - 1,)),
        ],
        compiler_params=pltpu.CompilerParams(
            collective_id=0, has_side_effects=True, vmem_limit_bytes=56 * 2**20
        ),
        name="project_and_sum",
    )(samples, whitening, traits, singular.reshape(1, k), lambdas)
    projected = projected.reshape(k, wide)
    tile = min(256, wide)
    return pl.pallas_call(
        functools.partial(fit_kernel, nl, nt),
        grid=(wide // tile,),
        out_shape=jax.ShapeDtypeStruct((nl, tall, wide), F32),
        in_specs=[
            pl.BlockSpec((nt, tall, own_k), lambda i: (0, 0, 0)),
            pl.BlockSpec((k, tile), lambda i: (0, i)),
            pl.BlockSpec((k, LANES), lambda i: (0, 0)),
            pl.BlockSpec((tall, LANES), lambda i: (0, 0)),
            pl.BlockSpec((tall, tile), lambda i: (0, i)),
        ],
        out_specs=pl.BlockSpec((nl, tall, tile), lambda i: (0, 0, i)),
        compiler_params=pltpu.CompilerParams(vmem_limit_bytes=60 * 2**20),
        name="fit",
    )(components, projected, shrink, leverage, traits)


def solution(mesh):
    n, nt = mesh.shape["samp"], mesh.shape["trait"]
    return jax.shard_map(
        functools.partial(local, n, nt),
        mesh=mesh,
        in_specs=(P("samp", None), P("samp", "trait"), P(None, "trait"), P(), P()),
        out_specs=P(None, "samp", "trait"),
        check_vma=False,
    )
```

```python
import functools

import jax
import jax.numpy as jnp
from jax import lax
from jax.experimental import pallas as pl
from jax.experimental.pallas import tpu as pltpu
from jax.sharding import PartitionSpec as P

MESH = pl.DeviceIdType.MESH
F32 = jnp.float32
BF16 = jnp.bfloat16
LANES = 128
ROWS = 16


WAVE = 6


def bit_orders(bits):
    rest = list(range(bits))
    if bits < 3:
        return [rest, rest[::-1]]
    a, b, c = [0, 1, 2] + rest[3:], [1, 2, 0] + rest[3:], [2, 0, 1] + rest[3:]
    return [a, b, c] * 5 + [[1, 0, 2] + rest[3:]]


def exchange_kernel(
    n, nt, nl, halves,
    s_hbm, w_hbm, y_hbm, sing_ref, lam_ref,
    c_ref, pj_ref, lev_ref, shr_ref,
    s_ref, w_ref, y_ref, acc, pb, rb,
    s_sem, w_sem, y_sem, rs_send, rs_recv, ag_send, ag_recv, c_send, c_recv,
):
    bits = n.bit_length() - 1
    units, unit, cols_of_unit = acc.shape
    own_k = c_ref.shape[2]
    own = own_k // unit
    block = min(unit, own_k)
    blocks = own_k // block
    orders = bit_orders(bits)
    me, mt = lax.axis_index("samp"), lax.axis_index("trait")
    value = [lax.rem(lax.div(me, 1 << b), 2) for b in range(bits)]
    peer = [me + (1 - 2 * value[b]) * (1 << b) for b in range(bits)]
    others = [lax.rem(mt + d, nt) for d in range(1, nt)]

    def w_copy(q):
        cols = slice(q * block, (q + 1) * block)
        return pltpu.make_async_copy(w_hbm.at[:, cols], w_ref.at[:, cols], w_sem.at[q])

    s_copy = pltpu.make_async_copy(s_hbm, s_ref, s_sem)
    y_copy = pltpu.make_async_copy(y_hbm, y_ref, y_sem)
    s_copy.start()
    w_copy(0).start()
    y_copy.start()
    for q in range(1, blocks):
        w_copy(q).start()

    barrier = pltpu.get_barrier_semaphore()
    for p in peer:
        pl.semaphore_signal(barrier, inc=1, device_id=(p, mt), device_id_type=MESH)
    for t in others:
        pl.semaphore_signal(barrier, inc=1, device_id=(me, t), device_id_type=MESH)

    def rows(start, size):
        return pl.ds(pl.multiple_of(start, ROWS), size)

    def order(s):
        return orders[s % len(orders)]

    keep, give = [], []
    for s in range(units):
        start, keeps, gives = 0, [], []
        for j, b in enumerate(order(s)):
            size = unit >> (j + 1)
            keeps.append(start + value[b] * size)
            gives.append(start + (1 - value[b]) * size)
            start = keeps[-1]
        keep.append(keeps)
        give.append(gives)

    def place(u):
        s, h = u // halves, u % halves
        if own:
            s = lax.rem(mt + s // own, nt) * own + s % own
        return s * halves + h

    def rs_copy(s, j):
        size = unit >> (j + 1)
        return pltpu.make_async_remote_copy(
            src_ref=pb.at[s, rows(give[s][j], size)],
            dst_ref=rb.at[s, pl.ds(unit - (unit >> j), size)],
            send_sem=rs_send.at[s, j],
            recv_sem=rs_recv.at[s, j],
            device_id=(peer[order(s)[j]], mt),
            device_id_type=MESH,
        )

    def ag_copy(s, j):
        size = unit >> (j + 1)
        held = pj_ref.at[place(s), rows(keep[s][j], size)]
        return pltpu.make_async_remote_copy(
            src_ref=held,
            dst_ref=held,
            send_sem=ag_send.at[s, j],
            recv_sem=ag_recv.at[s, j],
            device_id=(peer[order(s)[j]], mt),
            device_id_type=MESH,
        )

    def c_copy(d):
        return pltpu.make_async_remote_copy(
            src_ref=c_ref.at[mt],
            dst_ref=c_ref.at[mt],
            send_sem=c_send.at[d],
            recv_sem=c_recv.at[d],
            device_id=(me, others[d]),
            device_id_type=MESH,
        )

    contract_rows = (((0,), (0,)), ((), ()))

    def project(u):
        s, h = u // halves, u % halves
        right = y_ref[:, h * cols_of_unit:(h + 1) * cols_of_unit]
        if own:
            t = lax.rem(mt + s // own, nt)
            part = c_ref[t, :, (s % own) * unit:(s % own + 1) * unit]
            acc[u] = lax.dot_general(part, right, contract_rows, preferred_element_type=F32)
        else:
            pieces = unit // own_k
            for i in range(pieces):
                acc[u, i * own_k:(i + 1) * own_k, :] = lax.dot_general(
                    c_ref[s * pieces + i], right, contract_rows, preferred_element_type=F32
                )
        size = unit >> 1
        pb[u, rows(give[u][0], size), :] = acc[u, rows(give[u][0], size), :].astype(BF16)

    def own_block(q):
        cols = slice(q * block, (q + 1) * block)
        w_copy(q).wait()
        c_ref[mt, :, cols] = jnp.dot(
            s_ref[...], w_ref[:, cols], preferred_element_type=F32
        ).astype(BF16)
        if q == 0:
            pl.semaphore_wait(barrier, bits + nt - 1)
            y_copy.wait()
        if q == blocks - 1:
            for d in range(nt - 1):
                c_copy(d).start()

    def begin(u):
        s, h = u // halves, u % halves
        if u == 0:
            s_copy.wait()
        if h == 0:
            if own and s < own:
                own_block(s)
            elif not own and s == 0:
                for q in range(blocks):
                    own_block(q)
            if s == own:
                for d in range(nt - 1):
                    c_copy(d).wait_recv()
        project(u)
        rs_copy(u, 0).start()

    def halve(s, j):
        size = unit >> (j + 1)
        base = unit - (unit >> j)
        rs_copy(s, j).wait_recv()
        if j + 1 < bits:
            half = size >> 1
            first = give[s][j + 1]
            landed = rb[s, rows(base + first - keep[s][j], half), :].astype(F32)
            pb[s, rows(first, half), :] = (acc[s, rows(first, half), :] + landed).astype(BF16)
            rs_copy(s, j + 1).start()
            second = keep[s][j + 1]
            landed = rb[s, rows(base + second - keep[s][j], half), :].astype(F32)
            acc[s, rows(second, half), :] = acc[s, rows(second, half), :] + landed
        else:
            total = acc[s, rows(keep[s][j], size), :] + rb[s, base:base + size, :].astype(F32)
            pj_ref[place(s), rows(keep[s][j], size), :] = total.astype(BF16)
            ag_copy(s, j).start()

    def double(s, j):
        ag_copy(s, j).wait_recv()
        if j > 0:
            ag_copy(s, j - 1).start()

    def leverage():
        squared = sing_ref[...] * sing_ref[...]
        row = lax.broadcasted_iota(jnp.int32, (LANES, squared.shape[1]), 0)
        lam = jnp.full(row.shape, 1.0, F32)
        for l in range(nl):
            lam = jnp.where(row == l, lam_ref[l], lam)
        shrink = squared / (squared + lam)
        shr_ref[...] = shrink.T
        tall = c_ref.shape[1]
        step = min(64, tall)

        @pl.loop(0, tall // step)
        def _(i):
            here = pl.ds(pl.multiple_of(i * step, step), step)
            sums = [jnp.zeros((step, 1), F32) for _ in range(nl)]
            for t in range(nt):
                wide = c_ref[t, here, :].astype(F32)
                wide = wide * wide
                for l in range(nl):
                    weight = shrink[l:l + 1, t * own_k:(t + 1) * own_k]
                    sums[l] = sums[l] + jnp.sum(wide * weight, axis=1, keepdims=True)
            lane = lax.broadcasted_iota(jnp.int32, (step, LANES), 1)
            result = jnp.zeros((step, LANES), F32)
            for l in range(nl):
                result = jnp.where(lane == l, sums[l], result)
            lev_ref[here, :] = result

    waves = [range(s, min(s + WAVE, units)) for s in range(0, units, WAVE)]
    for k in range(2 * bits + len(waves)):
        for w, wave in reversed(list(enumerate(waves))):
            for s in wave:
                stage = k - w
                if stage == 0:
                    begin(s)
                elif 0 < stage <= bits:
                    halve(s, stage - 1)
                elif bits < stage <= 2 * bits:
                    double(s, 2 * bits - stage)
        if k == 2 * bits - 1:
            leverage()

    for d in range(nt - 1):
        c_copy(d).wait_send()
    for s in range(units):
        for j in range(bits):
            rs_copy(s, j).wait_send()
            ag_copy(s, j).wait_send()


def fit_kernel(nl, nt, c_ref, pj_ref, shr_ref, lev_ref, y_ref, out_ref):
    own_k = c_ref.shape[2]
    pj = pj_ref[...].reshape(nt * own_k, pj_ref.shape[2])
    target = y_ref[...].astype(F32)
    for l in range(nl):
        fitted = jnp.zeros(target.shape, F32)
        for t in range(nt):
            here = slice(t * own_k, (t + 1) * own_k)
            wide = pj[here, :].astype(F32)
            scaled = (shr_ref[here, l:l + 1] * wide).astype(BF16)
            fitted = fitted + jnp.dot(c_ref[t], scaled, preferred_element_type=F32)
        divisor = jnp.maximum(1.0 - lev_ref[:, l:l + 1], 0.25)
        out_ref[l] = (target - fitted) * (1.0 / divisor)


def local(n, nt, samples, traits, whitening, singular, lambdas):
    tall, k = samples.shape
    own_k = whitening.shape[1]
    wide = traits.shape[1]
    nl = lambdas.shape[0]
    bits = n.bit_length() - 1
    unit = ROWS << bits
    halves = 2 if wide % (2 * LANES) == 0 else 1
    cols = wide // halves
    blocks = max(own_k // unit, 1)
    rows = k // unit
    units = rows * halves
    vmem = pl.BlockSpec(memory_space=pltpu.VMEM)
    components, projected, leverage, shrink = pl.pallas_call(
        functools.partial(exchange_kernel, n, nt, nl, halves),
        out_shape=[
            jax.ShapeDtypeStruct((nt, tall, own_k), BF16),
            jax.ShapeDtypeStruct((units, unit, cols), BF16),
            jax.ShapeDtypeStruct((tall, LANES), F32),
            jax.ShapeDtypeStruct((k, LANES), F32),
        ],
        in_specs=[pl.BlockSpec(memory_space=pl.ANY)] * 3 + [vmem, pl.BlockSpec(memory_space=pltpu.SMEM)],
        out_specs=[vmem] * 4,
        scratch_shapes=[
            pltpu.VMEM(samples.shape, BF16),
            pltpu.VMEM(whitening.shape, BF16),
            pltpu.VMEM(traits.shape, BF16),
            pltpu.VMEM((units, unit, cols), F32),
            pltpu.VMEM((units, unit, cols), BF16),
            pltpu.VMEM((units, unit, cols), BF16),
            pltpu.SemaphoreType.DMA,
            pltpu.SemaphoreType.DMA((blocks,)),
            pltpu.SemaphoreType.DMA,
            pltpu.SemaphoreType.DMA((units, bits)),
            pltpu.SemaphoreType.DMA((units, bits)),
            pltpu.SemaphoreType.DMA((units, bits)),
            pltpu.SemaphoreType.DMA((units, bits)),
            pltpu.SemaphoreType.DMA((nt - 1,)),
            pltpu.SemaphoreType.DMA((nt - 1,)),
        ],
        compiler_params=pltpu.CompilerParams(
            collective_id=0, has_side_effects=True, vmem_limit_bytes=56 * 2**20
        ),
        name="project_and_sum",
    )(samples, whitening, traits, singular.reshape(1, k), lambdas)
    projected = projected.reshape(rows, halves, unit, cols)
    tile = min(256, cols)
    per = cols // tile
    return pl.pallas_call(
        functools.partial(fit_kernel, nl, nt),
        grid=(wide // tile,),
        out_shape=jax.ShapeDtypeStruct((nl, tall, wide), F32),
        in_specs=[
            pl.BlockSpec((nt, tall, own_k), lambda i: (0, 0, 0)),
            pl.BlockSpec((rows, None, unit, tile), lambda i: (0, i // per, 0, i % per)),
            pl.BlockSpec((k, LANES), lambda i: (0, 0)),
            pl.BlockSpec((tall, LANES), lambda i: (0, 0)),
            pl.BlockSpec((tall, tile), lambda i: (0, i)),
        ],
        out_specs=pl.BlockSpec((nl, tall, tile), lambda i: (0, 0, i)),
        compiler_params=pltpu.CompilerParams(vmem_limit_bytes=60 * 2**20),
        name="fit",
    )(components, projected, shrink, leverage, traits)


def solution(mesh):
    n, nt = mesh.shape["samp"], mesh.shape["trait"]
    return jax.shard_map(
        functools.partial(local, n, nt),
        mesh=mesh,
        in_specs=(P("samp", None), P("samp", "trait"), P(None, "trait"), P(), P()),
        out_specs=P(None, "samp", "trait"),
        check_vma=False,
    )
```

```python
import functools

import jax
import jax.numpy as jnp
from jax import lax
from jax.experimental import pallas as pl
from jax.experimental.pallas import tpu as pltpu
from jax.sharding import PartitionSpec as P

MESH = pl.DeviceIdType.MESH
F32 = jnp.float32
BF16 = jnp.bfloat16
LANES = 128
ROWS = 16


WAVE = 4


def bit_orders(bits):
    rest = list(range(bits))
    if bits < 3:
        return [rest, rest[::-1]]
    a, b, c = [0, 1, 2] + rest[3:], [1, 2, 0] + rest[3:], [2, 0, 1] + rest[3:]
    return [a, b, c] * 5 + [[1, 0, 2] + rest[3:]]


def exchange_kernel(
    n, nt, nl, halves,
    s_hbm, w_hbm, y_hbm, sing_ref, lam_ref,
    part_hbm, c_late, p_late, shr_late, lev_ref,
    s_ref, w_ref, y_ref, acc, pb, rb, c_ref, pj_ref, shr_ref, part, c_wave, scaled,
    part_sem, s_sem, w_sem, y_sem, rs_send, rs_recv, ag_send, ag_recv, c_send, c_recv,
):
    bits = n.bit_length() - 1
    units, unit, cols_of_unit = acc.shape
    own_k = c_ref.shape[2]
    own = own_k // unit
    block = min(unit, own_k)
    blocks = own_k // block
    orders = bit_orders(bits)
    me, mt = lax.axis_index("samp"), lax.axis_index("trait")
    value = [lax.rem(lax.div(me, 1 << b), 2) for b in range(bits)]
    peer = [me + (1 - 2 * value[b]) * (1 << b) for b in range(bits)]
    others = [lax.rem(mt + d, nt) for d in range(1, nt)]

    def w_copy(q):
        cols = slice(q * block, (q + 1) * block)
        return pltpu.make_async_copy(w_hbm.at[:, cols], w_ref.at[:, cols], w_sem.at[q])

    s_copy = pltpu.make_async_copy(s_hbm, s_ref, s_sem)
    y_copy = pltpu.make_async_copy(y_hbm, y_ref, y_sem)
    s_copy.start()
    w_copy(0).start()
    y_copy.start()
    for q in range(1, blocks):
        w_copy(q).start()

    barrier = pltpu.get_barrier_semaphore()
    for p in peer:
        pl.semaphore_signal(barrier, inc=1, device_id=(p, mt), device_id_type=MESH)
    for t in others:
        pl.semaphore_signal(barrier, inc=1, device_id=(me, t), device_id_type=MESH)

    def rows(start, size):
        return pl.ds(pl.multiple_of(start, ROWS), size)

    def order(s):
        return orders[s % len(orders)]

    keep, give = [], []
    for s in range(units):
        start, keeps, gives = 0, [], []
        for j, b in enumerate(order(s)):
            size = unit >> (j + 1)
            keeps.append(start + value[b] * size)
            gives.append(start + (1 - value[b]) * size)
            start = keeps[-1]
        keep.append(keeps)
        give.append(gives)

    def place(u):
        s, h = u // halves, u % halves
        if own:
            s = lax.rem(mt + s // own, nt) * own + s % own
        return s * halves + h

    def rs_copy(s, j):
        size = unit >> (j + 1)
        return pltpu.make_async_remote_copy(
            src_ref=pb.at[s, rows(give[s][j], size)],
            dst_ref=rb.at[s, pl.ds(unit - (unit >> j), size)],
            send_sem=rs_send.at[s, j],
            recv_sem=rs_recv.at[s, j],
            device_id=(peer[order(s)[j]], mt),
            device_id_type=MESH,
        )

    def ag_copy(s, j):
        size = unit >> (j + 1)
        held = pj_ref.at[place(s), rows(keep[s][j], size)]
        return pltpu.make_async_remote_copy(
            src_ref=held,
            dst_ref=held,
            send_sem=ag_send.at[s, j],
            recv_sem=ag_recv.at[s, j],
            device_id=(peer[order(s)[j]], mt),
            device_id_type=MESH,
        )

    def c_copy(d):
        return pltpu.make_async_remote_copy(
            src_ref=c_ref.at[mt],
            dst_ref=c_ref.at[mt],
            send_sem=c_send.at[d],
            recv_sem=c_recv.at[d],
            device_id=(me, others[d]),
            device_id_type=MESH,
        )

    contract_rows = (((0,), (0,)), ((), ()))

    def project(u):
        s, h = u // halves, u % halves
        right = y_ref[:, h * cols_of_unit:(h + 1) * cols_of_unit]
        if own:
            t = lax.rem(mt + s // own, nt)
            part = c_ref[t, :, (s % own) * unit:(s % own + 1) * unit]
            acc[u] = lax.dot_general(part, right, contract_rows, preferred_element_type=F32)
        else:
            pieces = unit // own_k
            for i in range(pieces):
                acc[u, i * own_k:(i + 1) * own_k, :] = lax.dot_general(
                    c_ref[s * pieces + i], right, contract_rows, preferred_element_type=F32
                )
        size = unit >> 1
        pb[u, rows(give[u][0], size), :] = acc[u, rows(give[u][0], size), :].astype(BF16)

    def own_block(q):
        cols = slice(q * block, (q + 1) * block)
        w_copy(q).wait()
        c_ref[mt, :, cols] = jnp.dot(
            s_ref[...], w_ref[:, cols], preferred_element_type=F32
        ).astype(BF16)
        if q == 0:
            pl.semaphore_wait(barrier, bits + nt - 1)
            y_copy.wait()
        if q == blocks - 1:
            for d in range(nt - 1):
                c_copy(d).start()

    def begin(u):
        s, h = u // halves, u % halves
        if u == 0:
            s_copy.wait()
        if h == 0:
            if own and s < own:
                own_block(s)
            elif not own and s == 0:
                for q in range(blocks):
                    own_block(q)
            if s == own:
                for d in range(nt - 1):
                    c_copy(d).wait_recv()
        project(u)
        rs_copy(u, 0).start()

    def halve(s, j):
        size = unit >> (j + 1)
        base = unit - (unit >> j)
        rs_copy(s, j).wait_recv()
        if j + 1 < bits:
            half = size >> 1
            first = give[s][j + 1]
            landed = rb[s, rows(base + first - keep[s][j], half), :].astype(F32)
            pb[s, rows(first, half), :] = (acc[s, rows(first, half), :] + landed).astype(BF16)
            rs_copy(s, j + 1).start()
            second = keep[s][j + 1]
            landed = rb[s, rows(base + second - keep[s][j], half), :].astype(F32)
            acc[s, rows(second, half), :] = acc[s, rows(second, half), :] + landed
        else:
            total = acc[s, rows(keep[s][j], size), :] + rb[s, base:base + size, :].astype(F32)
            pj_ref[place(s), rows(keep[s][j], size), :] = total.astype(BF16)
            ag_copy(s, j).start()

    def double(s, j):
        ag_copy(s, j).wait_recv()
        if j > 0:
            ag_copy(s, j - 1).start()

    def leverage():
        squared = sing_ref[...] * sing_ref[...]
        row = lax.broadcasted_iota(jnp.int32, (LANES, squared.shape[1]), 0)
        lam = jnp.full(row.shape, 1.0, F32)
        for l in range(nl):
            lam = jnp.where(row == l, lam_ref[l], lam)
        shrink = squared / (squared + lam)
        shr_ref[...] = shrink.T
        tall = c_ref.shape[1]
        step = min(64, tall)

        @pl.loop(0, tall // step)
        def _(i):
            here = pl.ds(pl.multiple_of(i * step, step), step)
            sums = [jnp.zeros((step, 1), F32) for _ in range(nl)]
            for t in range(nt):
                wide = c_ref[t, here, :].astype(F32)
                wide = wide * wide
                for l in range(nl):
                    weight = shrink[l:l + 1, t * own_k:(t + 1) * own_k]
                    sums[l] = sums[l] + jnp.sum(wide * weight, axis=1, keepdims=True)
            lane = lax.broadcasted_iota(jnp.int32, (step, LANES), 1)
            result = jnp.zeros((step, LANES), F32)
            for l in range(nl):
                result = jnp.where(lane == l, sums[l], result)
            lev_ref[here, :] = result

    waves = [range(u, min(u + WAVE, units)) for u in range(0, units, WAVE)]
    last = len(waves) - 1

    def blocks_of(wave):
        return range(wave[0] // halves, (wave[-1] + 1) // halves)

    def part_copy(l):
        return pltpu.make_async_copy(part.at[l], part_hbm.at[l], part_sem.at[l])

    def gather_columns(wave, target):
        for i, s in enumerate(blocks_of(wave)):
            if own:
                t = lax.rem(mt + s // own, nt)
                target[:, i * unit:(i + 1) * unit] = (
                    c_ref[t, :, (s % own) * unit:(s % own + 1) * unit]
                )
            else:
                pieces = unit // own_k
                for p in range(pieces):
                    at = i * unit + p * own_k
                    target[:, at:at + own_k] = c_ref[s * pieces + p]

    def shrink_rows(s):
        return pl.ds(pl.multiple_of(lax.div(place(s * halves), halves) * unit, ROWS), unit)

    def fit(w):
        wave = waves[w]
        gather_columns(wave, c_wave)
        for l in range(nl):
            for h in range(halves):
                for i, s in enumerate(blocks_of(wave)):
                    wide = pj_ref[place(s * halves + h)].astype(F32)
                    scaled[i * unit:(i + 1) * unit, :] = (
                        shr_ref[shrink_rows(s), l:l + 1] * wide
                    ).astype(BF16)
                cols = slice(h * cols_of_unit, (h + 1) * cols_of_unit)
                term = jnp.dot(c_wave[...], scaled[...], preferred_element_type=F32)
                if w == 0:
                    part[l, :, cols] = term
                else:
                    part[l, :, cols] = part[l, :, cols] + term
            if w == last - 1:
                part_copy(l).start()

    for k in range(2 * bits + len(waves)):
        for w, wave in reversed(list(enumerate(waves))):
            stage = k - w
            if stage == 2 * bits and w > 0:
                fit(w - 1)
            for u in wave:
                if stage == 0:
                    begin(u)
                elif 0 < stage <= bits:
                    halve(u, stage - 1)
                elif bits < stage <= 2 * bits:
                    double(u, 2 * bits - stage)
        if k == 2 * bits - 2:
            leverage()
            gather_columns(waves[last], c_late)
            for i, s in enumerate(blocks_of(waves[last])):
                shr_late[i * unit:(i + 1) * unit, :] = shr_ref[shrink_rows(s), :]
            if last == 0:
                part[...] = jnp.zeros_like(part)
                for l in range(nl):
                    part_copy(l).start()

    for i, s in enumerate(blocks_of(waves[last])):
        for h in range(halves):
            cols = slice(h * cols_of_unit, (h + 1) * cols_of_unit)
            p_late[i * unit:(i + 1) * unit, cols] = pj_ref[place(s * halves + h)]
    for l in range(nl):
        part_copy(l).wait()
    for d in range(nt - 1):
        c_copy(d).wait_send()
    for s in range(units):
        for j in range(bits):
            rs_copy(s, j).wait_send()
            ag_copy(s, j).wait_send()


def finish_kernel(nl, part_ref, c_ref, p_ref, shr_ref, lev_ref, y_ref, out_ref):
    target = y_ref[...].astype(F32)
    wide = p_ref[...].astype(F32)
    for l in range(nl):
        scaled = (shr_ref[:, l:l + 1] * wide).astype(BF16)
        fitted = part_ref[l] + jnp.dot(c_ref[...], scaled, preferred_element_type=F32)
        divisor = jnp.maximum(1.0 - lev_ref[:, l:l + 1], 0.25)
        out_ref[l] = (target - fitted) * (1.0 / divisor)


def local(n, nt, samples, traits, whitening, singular, lambdas):
    tall, k = samples.shape
    own_k = whitening.shape[1]
    wide = traits.shape[1]
    nl = lambdas.shape[0]
    bits = n.bit_length() - 1
    unit = ROWS << bits
    halves = 2 if wide % (2 * LANES) == 0 else 1
    cols = wide // halves
    blocks = max(own_k // unit, 1)
    rows = k // unit
    units = rows * halves
    late = ((units - 1) % WAVE + 1) // halves * unit
    wave_k = WAVE // halves * unit
    vmem = pl.BlockSpec(memory_space=pltpu.VMEM)
    partial, components, projected, shrink, leverage = pl.pallas_call(
        functools.partial(exchange_kernel, n, nt, nl, halves),
        out_shape=[
            jax.ShapeDtypeStruct((nl, tall, wide), F32),
            jax.ShapeDtypeStruct((tall, late), BF16),
            jax.ShapeDtypeStruct((late, wide), BF16),
            jax.ShapeDtypeStruct((late, LANES), F32),
            jax.ShapeDtypeStruct((tall, LANES), F32),
        ],
        in_specs=[pl.BlockSpec(memory_space=pl.ANY)] * 3 + [vmem, pl.BlockSpec(memory_space=pltpu.SMEM)],
        out_specs=[pl.BlockSpec(memory_space=pl.ANY)] + [vmem] * 4,
        scratch_shapes=[
            pltpu.VMEM(samples.shape, BF16),
            pltpu.VMEM(whitening.shape, BF16),
            pltpu.VMEM(traits.shape, BF16),
            pltpu.VMEM((units, unit, cols), F32),
            pltpu.VMEM((units, unit, cols), BF16),
            pltpu.VMEM((units, unit, cols), BF16),
            pltpu.VMEM((nt, tall, own_k), BF16),
            pltpu.VMEM((units, unit, cols), BF16),
            pltpu.VMEM((k, LANES), F32),
            pltpu.VMEM((nl, tall, wide), F32),
            pltpu.VMEM((tall, wave_k), BF16),
            pltpu.VMEM((wave_k, cols), BF16),
            pltpu.SemaphoreType.DMA((nl,)),
            pltpu.SemaphoreType.DMA,
            pltpu.SemaphoreType.DMA((blocks,)),
            pltpu.SemaphoreType.DMA,
            pltpu.SemaphoreType.DMA((units, bits)),
            pltpu.SemaphoreType.DMA((units, bits)),
            pltpu.SemaphoreType.DMA((units, bits)),
            pltpu.SemaphoreType.DMA((units, bits)),
            pltpu.SemaphoreType.DMA((nt - 1,)),
            pltpu.SemaphoreType.DMA((nt - 1,)),
        ],
        compiler_params=pltpu.CompilerParams(
            collective_id=0, has_side_effects=True, vmem_limit_bytes=56 * 2**20
        ),
        name="project_and_sum",
    )(samples, whitening, traits, singular.reshape(1, k), lambdas)
    tile = min(2 * LANES, wide)
    return pl.pallas_call(
        functools.partial(finish_kernel, nl),
        grid=(wide // tile,),
        out_shape=jax.ShapeDtypeStruct((nl, tall, wide), F32),
        in_specs=[
            pl.BlockSpec((nl, tall, tile), lambda i: (0, 0, i)),
            pl.BlockSpec((tall, late), lambda i: (0, 0)),
            pl.BlockSpec((late, tile), lambda i: (0, i)),
            pl.BlockSpec((late, LANES), lambda i: (0, 0)),
            pl.BlockSpec((tall, LANES), lambda i: (0, 0)),
            pl.BlockSpec((tall, tile), lambda i: (0, i)),
        ],
        out_specs=pl.BlockSpec((nl, tall, tile), lambda i: (0, 0, i)),
        compiler_params=pltpu.CompilerParams(vmem_limit_bytes=60 * 2**20),
        name="finish",
    )(partial, components, projected, shrink, leverage, traits)


def solution(mesh):
    n, nt = mesh.shape["samp"], mesh.shape["trait"]
    return jax.shard_map(
        functools.partial(local, n, nt),
        mesh=mesh,
        in_specs=(P("samp", None), P("samp", "trait"), P(None, "trait"), P(), P()),
        out_specs=P(None, "samp", "trait"),
        check_vma=False,
    )
```

```python
import functools

import jax
import jax.numpy as jnp
from jax import lax
from jax.experimental import pallas as pl
from jax.experimental.pallas import tpu as pltpu
from jax.sharding import PartitionSpec as P

MESH = pl.DeviceIdType.MESH
F32 = jnp.float32
BF16 = jnp.bfloat16
LANES = 128
ROWS = 16


WAVE = 4


EARLY = -99


def wave_plan(bits, units):
    rest = list(range(bits))
    if bits < 3:
        orders = [rest, rest[::-1]]
    else:
        a, b, c = [0, 1, 2] + rest[3:], [1, 2, 0] + rest[3:], [2, 0, 1] + rest[3:]
        orders = [a, b, c] * 5 + [[1, 0, 2] + rest[3:]]
    waves = [list(range(u, min(u + WAVE, units))) for u in range(0, units, WAVE)]
    plan = []
    for k in range(2 * bits + len(waves)):
        for w in reversed(range(len(waves))):
            if k - w == 2 * bits and w > 0:
                plan.append(-w)
            if 0 <= k - w <= 2 * bits:
                plan += waves[w]
        if k == 2 * bits - 2:
            plan.append(EARLY)
    return [orders[u % len(orders)] for u in range(units)], plan


PLANS = {
    (4, 16): ([
        [0, 1, 2, 3], [1, 0, 2, 3], [0, 1, 2, 3], [2, 1, 0, 3],
        [1, 2, 0, 3], [0, 1, 2, 3], [2, 1, 0, 3], [0, 1, 2, 3],
        [0, 1, 2, 3], [2, 1, 0, 3], [1, 2, 0, 3], [2, 1, 0, 3],
        [0, 1, 2, 3], [1, 0, 2, 3], [0, 1, 2, 3], [0, 1, 2, 3],
    ], [
        0, 1, 2, 3, 4, 5, 6, 0, 1, 7, 8, 9, 2, 10, 4, 5, 11, 12, 7, 3, 2, 0, 13, 4, 1, 10, 14, 5, 2, 7, 0, 8,
        1, 3, 4, 6, 15, 5, 9, 2, 7, 10, 0, 14, 3, 1, 11, 8, 6, 5, 2, 4, 9, 7, 0, 12, 15, 3, 14, 6, 5, 10, 11,
        4, 9, 13, 1, 8, 7, 2, 3, 14, 0, 12, 6, 15, 11, 1, 9, 5, 8, 13, 2, 14, 3, 10, 6, 15, 4, 12, 0, 7, 8,
        1, 11, 14, 13, 9, 15, 6, 10, 3, 8, 11, 5, 14, 7, 13, 9, 4, 15, 1, 12, 10, 6, EARLY, 14, 13, 11, 0,
        15, 2, 3, 12, 5, 8, 9, 10, -1, 13, 6, 12, 7, 4, 11, 15, -2, 13, 12, 8, 9, 10, 14, 11, -3, 15, 13, 12,
    ]),
}


def make_plan(bits, units):
    return PLANS.get((bits, units)) or wave_plan(bits, units)


def exchange_kernel(
    n, nt, nl, halves,
    s_hbm, w_hbm, y_hbm, sing_ref, lam_ref,
    part_hbm, c_late, p_late, shr_late, lev_ref,
    s_ref, w_ref, y_ref, acc, pb, rb, c_ref, pj_ref, shr_ref, part, c_wave, scaled,
    part_sem, s_sem, w_sem, y_sem, rs_send, rs_recv, ag_send, ag_recv, c_send, c_recv,
):
    bits = n.bit_length() - 1
    units, unit, cols_of_unit = acc.shape
    own_k = c_ref.shape[2]
    own = own_k // unit
    block = min(unit, own_k)
    blocks = own_k // block
    orders, plan = make_plan(bits, units)
    me, mt = lax.axis_index("samp"), lax.axis_index("trait")
    value = [lax.rem(lax.div(me, 1 << b), 2) for b in range(bits)]
    peer = [me + (1 - 2 * value[b]) * (1 << b) for b in range(bits)]
    others = [lax.rem(mt + d, nt) for d in range(1, nt)]

    def w_copy(q):
        cols = slice(q * block, (q + 1) * block)
        return pltpu.make_async_copy(w_hbm.at[:, cols], w_ref.at[:, cols], w_sem.at[q])

    s_copy = pltpu.make_async_copy(s_hbm, s_ref, s_sem)
    y_copy = pltpu.make_async_copy(y_hbm, y_ref, y_sem)
    s_copy.start()
    w_copy(0).start()
    y_copy.start()
    for q in range(1, blocks):
        w_copy(q).start()

    barrier = pltpu.get_barrier_semaphore()
    for p in peer:
        pl.semaphore_signal(barrier, inc=1, device_id=(p, mt), device_id_type=MESH)
    for t in others:
        pl.semaphore_signal(barrier, inc=1, device_id=(me, t), device_id_type=MESH)

    def rows(start, size):
        return pl.ds(pl.multiple_of(start, ROWS), size)

    def order(s):
        return orders[s]

    keep, give = [], []
    for s in range(units):
        start, keeps, gives = 0, [], []
        for j, b in enumerate(order(s)):
            size = unit >> (j + 1)
            keeps.append(start + value[b] * size)
            gives.append(start + (1 - value[b]) * size)
            start = keeps[-1]
        keep.append(keeps)
        give.append(gives)

    def place(u):
        s, h = u // halves, u % halves
        if own:
            s = lax.rem(mt + s // own, nt) * own + s % own
        return s * halves + h

    def rs_copy(s, j):
        size = unit >> (j + 1)
        return pltpu.make_async_remote_copy(
            src_ref=pb.at[s, rows(give[s][j], size)],
            dst_ref=rb.at[s, pl.ds(unit - (unit >> j), size)],
            send_sem=rs_send.at[s, j],
            recv_sem=rs_recv.at[s, j],
            device_id=(peer[order(s)[j]], mt),
            device_id_type=MESH,
        )

    def ag_copy(s, j):
        size = unit >> (j + 1)
        held = pj_ref.at[place(s), rows(keep[s][j], size)]
        return pltpu.make_async_remote_copy(
            src_ref=held,
            dst_ref=held,
            send_sem=ag_send.at[s, j],
            recv_sem=ag_recv.at[s, j],
            device_id=(peer[order(s)[j]], mt),
            device_id_type=MESH,
        )

    def c_copy(d):
        return pltpu.make_async_remote_copy(
            src_ref=c_ref.at[mt],
            dst_ref=c_ref.at[mt],
            send_sem=c_send.at[d],
            recv_sem=c_recv.at[d],
            device_id=(me, others[d]),
            device_id_type=MESH,
        )

    contract_rows = (((0,), (0,)), ((), ()))

    def project(u):
        s, h = u // halves, u % halves
        right = y_ref[:, h * cols_of_unit:(h + 1) * cols_of_unit]
        if own:
            t = lax.rem(mt + s // own, nt)
            part = c_ref[t, :, (s % own) * unit:(s % own + 1) * unit]
            acc[u] = lax.dot_general(part, right, contract_rows, preferred_element_type=F32)
        else:
            pieces = unit // own_k
            for i in range(pieces):
                acc[u, i * own_k:(i + 1) * own_k, :] = lax.dot_general(
                    c_ref[s * pieces + i], right, contract_rows, preferred_element_type=F32
                )
        size = unit >> 1
        pb[u, rows(give[u][0], size), :] = acc[u, rows(give[u][0], size), :].astype(BF16)

    def own_block(q):
        cols = slice(q * block, (q + 1) * block)
        w_copy(q).wait()
        c_ref[mt, :, cols] = jnp.dot(
            s_ref[...], w_ref[:, cols], preferred_element_type=F32
        ).astype(BF16)
        if q == 0:
            pl.semaphore_wait(barrier, bits + nt - 1)
            y_copy.wait()
        if q == blocks - 1:
            for d in range(nt - 1):
                c_copy(d).start()

    def begin(u):
        s, h = u // halves, u % halves
        if u == 0:
            s_copy.wait()
        if h == 0:
            if own and s < own:
                own_block(s)
            elif not own and s == 0:
                for q in range(blocks):
                    own_block(q)
            if s == own:
                for d in range(nt - 1):
                    c_copy(d).wait_recv()
        project(u)
        rs_copy(u, 0).start()

    def halve(s, j):
        size = unit >> (j + 1)
        base = unit - (unit >> j)
        rs_copy(s, j).wait_recv()
        if j + 1 < bits:
            half = size >> 1
            first = give[s][j + 1]
            landed = rb[s, rows(base + first - keep[s][j], half), :].astype(F32)
            pb[s, rows(first, half), :] = (acc[s, rows(first, half), :] + landed).astype(BF16)
            rs_copy(s, j + 1).start()
            second = keep[s][j + 1]
            landed = rb[s, rows(base + second - keep[s][j], half), :].astype(F32)
            acc[s, rows(second, half), :] = acc[s, rows(second, half), :] + landed
        else:
            total = acc[s, rows(keep[s][j], size), :] + rb[s, base:base + size, :].astype(F32)
            pj_ref[place(s), rows(keep[s][j], size), :] = total.astype(BF16)
            ag_copy(s, j).start()

    def double(s, j):
        ag_copy(s, j).wait_recv()
        if j > 0:
            ag_copy(s, j - 1).start()

    def leverage():
        squared = sing_ref[...] * sing_ref[...]
        row = lax.broadcasted_iota(jnp.int32, (LANES, squared.shape[1]), 0)
        lam = jnp.full(row.shape, 1.0, F32)
        for l in range(nl):
            lam = jnp.where(row == l, lam_ref[l], lam)
        shrink = squared / (squared + lam)
        shr_ref[...] = shrink.T
        tall = c_ref.shape[1]
        step = min(64, tall)

        @pl.loop(0, tall // step)
        def _(i):
            here = pl.ds(pl.multiple_of(i * step, step), step)
            sums = [jnp.zeros((step, 1), F32) for _ in range(nl)]
            for t in range(nt):
                wide = c_ref[t, here, :].astype(F32)
                wide = wide * wide
                for l in range(nl):
                    weight = shrink[l:l + 1, t * own_k:(t + 1) * own_k]
                    sums[l] = sums[l] + jnp.sum(wide * weight, axis=1, keepdims=True)
            lane = lax.broadcasted_iota(jnp.int32, (step, LANES), 1)
            result = jnp.zeros((step, LANES), F32)
            for l in range(nl):
                result = jnp.where(lane == l, sums[l], result)
            lev_ref[here, :] = result

    waves = [range(u, min(u + WAVE, units)) for u in range(0, units, WAVE)]
    last = len(waves) - 1

    def blocks_of(wave):
        return range(wave[0] // halves, (wave[-1] + 1) // halves)

    def part_copy(l):
        return pltpu.make_async_copy(part.at[l], part_hbm.at[l], part_sem.at[l])

    def gather_columns(wave, target):
        for i, s in enumerate(blocks_of(wave)):
            if own:
                t = lax.rem(mt + s // own, nt)
                target[:, i * unit:(i + 1) * unit] = (
                    c_ref[t, :, (s % own) * unit:(s % own + 1) * unit]
                )
            else:
                pieces = unit // own_k
                for p in range(pieces):
                    at = i * unit + p * own_k
                    target[:, at:at + own_k] = c_ref[s * pieces + p]

    def shrink_rows(s):
        return pl.ds(pl.multiple_of(lax.div(place(s * halves), halves) * unit, ROWS), unit)

    def fit(w, first, final):
        wave = waves[w]
        gather_columns(wave, c_wave)
        for l in range(nl):
            for h in range(halves):
                for i, s in enumerate(blocks_of(wave)):
                    wide = pj_ref[place(s * halves + h)].astype(F32)
                    scaled[i * unit:(i + 1) * unit, :] = (
                        shr_ref[shrink_rows(s), l:l + 1] * wide
                    ).astype(BF16)
                cols = slice(h * cols_of_unit, (h + 1) * cols_of_unit)
                term = jnp.dot(c_wave[...], scaled[...], preferred_element_type=F32)
                if first:
                    part[l, :, cols] = term
                else:
                    part[l, :, cols] = part[l, :, cols] + term
            if final:
                part_copy(l).start()

    def early():
        leverage()
        gather_columns(waves[last], c_late)
        for i, s in enumerate(blocks_of(waves[last])):
            shr_late[i * unit:(i + 1) * unit, :] = shr_ref[shrink_rows(s), :]
        if last == 0:
            part[...] = jnp.zeros_like(part)
            for l in range(nl):
                part_copy(l).start()

    stage = [0] * units
    fits = 0
    for u in plan:
        if u == EARLY:
            early()
        elif u < 0:
            fits += 1
            fit(-1 - u, fits == 1, fits == last)
        else:
            if stage[u] == 0:
                begin(u)
            elif stage[u] <= bits:
                halve(u, stage[u] - 1)
            else:
                double(u, 2 * bits - stage[u])
            stage[u] += 1

    for i, s in enumerate(blocks_of(waves[last])):
        for h in range(halves):
            cols = slice(h * cols_of_unit, (h + 1) * cols_of_unit)
            p_late[i * unit:(i + 1) * unit, cols] = pj_ref[place(s * halves + h)]
    for l in range(nl):
        part_copy(l).wait()
    for d in range(nt - 1):
        c_copy(d).wait_send()
    for s in range(units):
        for j in range(bits):
            rs_copy(s, j).wait_send()
            ag_copy(s, j).wait_send()


def finish_kernel(nl, part_ref, c_ref, p_ref, shr_ref, lev_ref, y_ref, out_ref):
    target = y_ref[...].astype(F32)
    wide = p_ref[...].astype(F32)
    for l in range(nl):
        scaled = (shr_ref[:, l:l + 1] * wide).astype(BF16)
        fitted = part_ref[l] + jnp.dot(c_ref[...], scaled, preferred_element_type=F32)
        divisor = jnp.maximum(1.0 - lev_ref[:, l:l + 1], 0.25)
        out_ref[l] = (target - fitted) * (1.0 / divisor)


def local(n, nt, samples, traits, whitening, singular, lambdas):
    tall, k = samples.shape
    own_k = whitening.shape[1]
    wide = traits.shape[1]
    nl = lambdas.shape[0]
    bits = n.bit_length() - 1
    unit = ROWS << bits
    halves = 2 if wide % (2 * LANES) == 0 else 1
    cols = wide // halves
    blocks = max(own_k // unit, 1)
    rows = k // unit
    units = rows * halves
    late = ((units - 1) % WAVE + 1) // halves * unit
    wave_k = WAVE // halves * unit
    vmem = pl.BlockSpec(memory_space=pltpu.VMEM)
    partial, components, projected, shrink, leverage = pl.pallas_call(
        functools.partial(exchange_kernel, n, nt, nl, halves),
        out_shape=[
            jax.ShapeDtypeStruct((nl, tall, wide), F32),
            jax.ShapeDtypeStruct((tall, late), BF16),
            jax.ShapeDtypeStruct((late, wide), BF16),
            jax.ShapeDtypeStruct((late, LANES), F32),
            jax.ShapeDtypeStruct((tall, LANES), F32),
        ],
        in_specs=[pl.BlockSpec(memory_space=pl.ANY)] * 3 + [vmem, pl.BlockSpec(memory_space=pltpu.SMEM)],
        out_specs=[pl.BlockSpec(memory_space=pl.ANY)] + [vmem] * 4,
        scratch_shapes=[
            pltpu.VMEM(samples.shape, BF16),
            pltpu.VMEM(whitening.shape, BF16),
            pltpu.VMEM(traits.shape, BF16),
            pltpu.VMEM((units, unit, cols), F32),
            pltpu.VMEM((units, unit, cols), BF16),
            pltpu.VMEM((units, unit, cols), BF16),
            pltpu.VMEM((nt, tall, own_k), BF16),
            pltpu.VMEM((units, unit, cols), BF16),
            pltpu.VMEM((k, LANES), F32),
            pltpu.VMEM((nl, tall, wide), F32),
            pltpu.VMEM((tall, wave_k), BF16),
            pltpu.VMEM((wave_k, cols), BF16),
            pltpu.SemaphoreType.DMA((nl,)),
            pltpu.SemaphoreType.DMA,
            pltpu.SemaphoreType.DMA((blocks,)),
            pltpu.SemaphoreType.DMA,
            pltpu.SemaphoreType.DMA((units, bits)),
            pltpu.SemaphoreType.DMA((units, bits)),
            pltpu.SemaphoreType.DMA((units, bits)),
            pltpu.SemaphoreType.DMA((units, bits)),
            pltpu.SemaphoreType.DMA((nt - 1,)),
            pltpu.SemaphoreType.DMA((nt - 1,)),
        ],
        compiler_params=pltpu.CompilerParams(
            collective_id=0, has_side_effects=True, vmem_limit_bytes=56 * 2**20
        ),
        name="project_and_sum",
    )(samples, whitening, traits, singular.reshape(1, k), lambdas)
    tile = min(2 * LANES, wide)
    return pl.pallas_call(
        functools.partial(finish_kernel, nl),
        grid=(wide // tile,),
        out_shape=jax.ShapeDtypeStruct((nl, tall, wide), F32),
        in_specs=[
            pl.BlockSpec((nl, tall, tile), lambda i: (0, 0, i)),
            pl.BlockSpec((tall, late), lambda i: (0, 0)),
            pl.BlockSpec((late, tile), lambda i: (0, i)),
            pl.BlockSpec((late, LANES), lambda i: (0, 0)),
            pl.BlockSpec((tall, LANES), lambda i: (0, 0)),
            pl.BlockSpec((tall, tile), lambda i: (0, i)),
        ],
        out_specs=pl.BlockSpec((nl, tall, tile), lambda i: (0, 0, i)),
        compiler_params=pltpu.CompilerParams(vmem_limit_bytes=60 * 2**20),
        name="finish",
    )(partial, components, projected, shrink, leverage, traits)


def solution(mesh):
    n, nt = mesh.shape["samp"], mesh.shape["trait"]
    return jax.shard_map(
        functools.partial(local, n, nt),
        mesh=mesh,
        in_specs=(P("samp", None), P("samp", "trait"), P(None, "trait"), P(), P()),
        out_specs=P(None, "samp", "trait"),
        check_vma=False,
    )
```

```python
import functools

import jax
import jax.numpy as jnp
from jax import lax
from jax.experimental import pallas as pl
from jax.experimental.pallas import tpu as pltpu
from jax.sharding import PartitionSpec as P

MESH = pl.DeviceIdType.MESH
F32 = jnp.float32
BF16 = jnp.bfloat16
LANES = 128
ROWS = 16


WAVE = 4


EARLY = -99


def wave_plan(bits, units):
    rest = list(range(bits))
    if bits < 3:
        orders = [rest, rest[::-1]]
    else:
        a, b, c = [0, 1, 2] + rest[3:], [1, 2, 0] + rest[3:], [2, 0, 1] + rest[3:]
        orders = [a, b, c] * 5 + [[1, 0, 2] + rest[3:]]
    waves = [list(range(u, min(u + WAVE, units))) for u in range(0, units, WAVE)]
    plan = []
    for k in range(2 * bits + len(waves)):
        for w in reversed(range(len(waves))):
            if k - w == 2 * bits and w > 0:
                plan.append(-w)
            if 0 <= k - w <= 2 * bits:
                plan += waves[w]
        if k == 2 * bits - 2:
            plan.append(EARLY)
    return [orders[u % len(orders)] for u in range(units)], plan


PLANS = {
    (4, 16): ([
        [0, 1, 2, 3], [1, 0, 2, 3], [0, 1, 2, 3], [2, 1, 0, 3],
        [1, 2, 0, 3], [0, 1, 2, 3], [2, 1, 0, 3], [0, 1, 2, 3],
        [0, 1, 2, 3], [2, 1, 0, 3], [1, 2, 0, 3], [2, 1, 0, 3],
        [0, 1, 2, 3], [1, 0, 2, 3], [0, 1, 2, 3], [0, 1, 2, 3],
    ], [
        0, 1, 2, 3, 4, 5, 6, 0, 1, 7, 8, 9, 2, 10, 4, 5, 11, 12, 7, 3, 2, 0, 13, 4, 1, 10, 14, 5, 2, 7, 0, 8,
        1, 3, 4, 6, 15, 5, 9, 2, 7, 10, 0, 14, 3, 1, 11, 8, 6, 5, 2, 4, 9, 7, 0, 12, 15, 3, 14, 6, 5, 10, 11,
        4, 9, 13, 1, 8, 7, 2, 3, 14, 0, 12, 6, 15, 11, 1, 9, 5, 8, 13, 2, 14, 3, 10, 6, 15, 4, 12, 0, 7, 8,
        1, 11, 14, 13, 9, 15, 6, 10, 3, 8, 11, 5, 14, 7, 13, 9, 4, 15, 1, 12, 10, 6, EARLY, 14, 13, 11, 0,
        15, 2, 3, 12, 5, 8, 9, 10, -1, 13, 6, 12, 7, 4, 11, 15, -2, 13, 12, 8, 9, 10, 14, 11, -3, 15, 13, 12,
    ]),
}


def make_plan(bits, units):
    return PLANS.get((bits, units)) or wave_plan(bits, units)


def exchange_kernel(
    n, nt, nl, halves,
    s_hbm, w_hbm, y_hbm, sing_ref, lam_ref,
    part_hbm, c_late, p_late, shr_late, inv_ref,
    s_ref, w_ref, y_ref, acc, pb, rb, c_ref, pj_ref, shr_ref, part, c_wave, scaled,
    part_sem, s_sem, w_sem, y_sem, rs_send, rs_recv, ag_send, ag_recv, c_send, c_recv,
):
    bits = n.bit_length() - 1
    units, unit, cols_of_unit = acc.shape
    own_k = c_ref.shape[2]
    own = own_k // unit
    block = min(unit, own_k)
    blocks = own_k // block
    orders, plan = make_plan(bits, units)
    me, mt = lax.axis_index("samp"), lax.axis_index("trait")
    value = [lax.rem(lax.div(me, 1 << b), 2) for b in range(bits)]
    peer = [me + (1 - 2 * value[b]) * (1 << b) for b in range(bits)]
    others = [lax.rem(mt + d, nt) for d in range(1, nt)]

    def w_copy(q):
        cols = slice(q * block, (q + 1) * block)
        return pltpu.make_async_copy(w_hbm.at[:, cols], w_ref.at[:, cols], w_sem.at[q])

    s_copy = pltpu.make_async_copy(s_hbm, s_ref, s_sem)
    y_copy = pltpu.make_async_copy(y_hbm, y_ref, y_sem)
    s_copy.start()
    w_copy(0).start()
    y_copy.start()
    for q in range(1, blocks):
        w_copy(q).start()

    barrier = pltpu.get_barrier_semaphore()
    for p in peer:
        pl.semaphore_signal(barrier, inc=1, device_id=(p, mt), device_id_type=MESH)
    for t in others:
        pl.semaphore_signal(barrier, inc=1, device_id=(me, t), device_id_type=MESH)

    def rows(start, size):
        return pl.ds(pl.multiple_of(start, ROWS), size)

    def order(s):
        return orders[s]

    keep, give = [], []
    for s in range(units):
        start, keeps, gives = 0, [], []
        for j, b in enumerate(order(s)):
            size = unit >> (j + 1)
            keeps.append(start + value[b] * size)
            gives.append(start + (1 - value[b]) * size)
            start = keeps[-1]
        keep.append(keeps)
        give.append(gives)

    def place(u):
        s, h = u // halves, u % halves
        if own:
            s = lax.rem(mt + s // own, nt) * own + s % own
        return s * halves + h

    def rs_copy(s, j):
        size = unit >> (j + 1)
        return pltpu.make_async_remote_copy(
            src_ref=pb.at[s, rows(give[s][j], size)],
            dst_ref=rb.at[s, pl.ds(unit - (unit >> j), size)],
            send_sem=rs_send.at[s, j],
            recv_sem=rs_recv.at[s, j],
            device_id=(peer[order(s)[j]], mt),
            device_id_type=MESH,
        )

    def ag_copy(s, j):
        size = unit >> (j + 1)
        held = pj_ref.at[place(s), rows(keep[s][j], size)]
        return pltpu.make_async_remote_copy(
            src_ref=held,
            dst_ref=held,
            send_sem=ag_send.at[s, j],
            recv_sem=ag_recv.at[s, j],
            device_id=(peer[order(s)[j]], mt),
            device_id_type=MESH,
        )

    def c_copy(d):
        return pltpu.make_async_remote_copy(
            src_ref=c_ref.at[mt],
            dst_ref=c_ref.at[mt],
            send_sem=c_send.at[d],
            recv_sem=c_recv.at[d],
            device_id=(me, others[d]),
            device_id_type=MESH,
        )

    contract_rows = (((0,), (0,)), ((), ()))

    def project(u):
        s, h = u // halves, u % halves
        right = y_ref[:, h * cols_of_unit:(h + 1) * cols_of_unit]
        if own:
            t = lax.rem(mt + s // own, nt)
            part = c_ref[t, :, (s % own) * unit:(s % own + 1) * unit]
            acc[u] = lax.dot_general(part, right, contract_rows, preferred_element_type=F32)
        else:
            pieces = unit // own_k
            for i in range(pieces):
                acc[u, i * own_k:(i + 1) * own_k, :] = lax.dot_general(
                    c_ref[s * pieces + i], right, contract_rows, preferred_element_type=F32
                )
        size = unit >> 1
        pb[u, rows(give[u][0], size), :] = acc[u, rows(give[u][0], size), :].astype(BF16)

    def own_block(q):
        cols = slice(q * block, (q + 1) * block)
        w_copy(q).wait()
        c_ref[mt, :, cols] = jnp.dot(
            s_ref[...], w_ref[:, cols], preferred_element_type=F32
        ).astype(BF16)
        if q == 0:
            pl.semaphore_wait(barrier, bits + nt - 1)
            y_copy.wait()
        if q == blocks - 1:
            for d in range(nt - 1):
                c_copy(d).start()

    def begin(u):
        s, h = u // halves, u % halves
        if u == 0:
            s_copy.wait()
        if h == 0:
            if own and s < own:
                own_block(s)
            elif not own and s == 0:
                for q in range(blocks):
                    own_block(q)
            if s == own:
                for d in range(nt - 1):
                    c_copy(d).wait_recv()
        project(u)
        rs_copy(u, 0).start()

    def halve(s, j):
        size = unit >> (j + 1)
        base = unit - (unit >> j)
        rs_copy(s, j).wait_recv()
        if j + 1 < bits:
            half = size >> 1
            first = give[s][j + 1]
            landed = rb[s, rows(base + first - keep[s][j], half), :].astype(F32)
            pb[s, rows(first, half), :] = (acc[s, rows(first, half), :] + landed).astype(BF16)
            rs_copy(s, j + 1).start()
            second = keep[s][j + 1]
            landed = rb[s, rows(base + second - keep[s][j], half), :].astype(F32)
            acc[s, rows(second, half), :] = acc[s, rows(second, half), :] + landed
        else:
            total = acc[s, rows(keep[s][j], size), :] + rb[s, base:base + size, :].astype(F32)
            pj_ref[place(s), rows(keep[s][j], size), :] = total.astype(BF16)
            ag_copy(s, j).start()

    def double(s, j):
        ag_copy(s, j).wait_recv()
        if j > 0:
            ag_copy(s, j - 1).start()

    def leverage():
        squared = sing_ref[...] * sing_ref[...]
        row = lax.broadcasted_iota(jnp.int32, (LANES, squared.shape[1]), 0)
        lam = jnp.full(row.shape, 1.0, F32)
        for l in range(nl):
            lam = jnp.where(row == l, lam_ref[l], lam)
        shrink = squared / (squared + lam)
        shr_ref[...] = shrink.T
        tall = c_ref.shape[1]
        step = min(64, tall)

        @pl.loop(0, tall // step)
        def _(i):
            here = pl.ds(pl.multiple_of(i * step, step), step)
            sums = [jnp.zeros((step, 1), F32) for _ in range(nl)]
            for t in range(nt):
                wide = c_ref[t, here, :].astype(F32)
                wide = wide * wide
                for l in range(nl):
                    weight = shrink[l:l + 1, t * own_k:(t + 1) * own_k]
                    sums[l] = sums[l] + jnp.sum(wide * weight, axis=1, keepdims=True)
            lane = lax.broadcasted_iota(jnp.int32, (step, LANES), 1)
            result = jnp.zeros((step, LANES), F32)
            for l in range(nl):
                result = jnp.where(lane == l, sums[l], result)
            inv_ref[here, :] = 1.0 / jnp.maximum(1.0 - result, 0.25)

    waves = [range(u, min(u + WAVE, units)) for u in range(0, units, WAVE)]
    last = len(waves) - 1

    def blocks_of(wave):
        return range(wave[0] // halves, (wave[-1] + 1) // halves)

    def part_copy(l):
        return pltpu.make_async_copy(part.at[l], part_hbm.at[l], part_sem.at[l])

    def gather_columns(wave, target):
        for i, s in enumerate(blocks_of(wave)):
            if own:
                t = lax.rem(mt + s // own, nt)
                target[:, i * unit:(i + 1) * unit] = (
                    c_ref[t, :, (s % own) * unit:(s % own + 1) * unit]
                )
            else:
                pieces = unit // own_k
                for p in range(pieces):
                    at = i * unit + p * own_k
                    target[:, at:at + own_k] = c_ref[s * pieces + p]

    def shrink_rows(s):
        return pl.ds(pl.multiple_of(lax.div(place(s * halves), halves) * unit, ROWS), unit)

    def fit(w, first, final):
        wave = waves[w]
        gather_columns(wave, c_wave)
        for l in range(nl):
            for h in range(halves):
                for i, s in enumerate(blocks_of(wave)):
                    wide = pj_ref[place(s * halves + h)].astype(F32)
                    scaled[i * unit:(i + 1) * unit, :] = (
                        shr_ref[shrink_rows(s), l:l + 1] * wide
                    ).astype(BF16)
                cols = slice(h * cols_of_unit, (h + 1) * cols_of_unit)
                term = jnp.dot(c_wave[...], scaled[...], preferred_element_type=F32)
                base = y_ref[:, cols].astype(F32) if first else part[l, :, cols]
                rest = base - term
                part[l, :, cols] = rest * inv_ref[:, l:l + 1] if final else rest
            if final:
                part_copy(l).start()

    def early():
        leverage()
        gather_columns(waves[last], c_late)
        for i, s in enumerate(blocks_of(waves[last])):
            shr_late[i * unit:(i + 1) * unit, :] = shr_ref[shrink_rows(s), :]
        if last == 0:
            for l in range(nl):
                part[l] = y_ref[...].astype(F32) * inv_ref[:, l:l + 1]
                part_copy(l).start()

    stage = [0] * units
    fits = 0
    for u in plan:
        if u == EARLY:
            early()
        elif u < 0:
            fits += 1
            fit(-1 - u, fits == 1, fits == last)
        else:
            if stage[u] == 0:
                begin(u)
            elif stage[u] <= bits:
                halve(u, stage[u] - 1)
            else:
                double(u, 2 * bits - stage[u])
            stage[u] += 1

    for i, s in enumerate(blocks_of(waves[last])):
        for h in range(halves):
            cols = slice(h * cols_of_unit, (h + 1) * cols_of_unit)
            p_late[i * unit:(i + 1) * unit, cols] = pj_ref[place(s * halves + h)]
    for l in range(nl):
        part_copy(l).wait()
    for d in range(nt - 1):
        c_copy(d).wait_send()
    for s in range(units):
        for j in range(bits):
            rs_copy(s, j).wait_send()
            ag_copy(s, j).wait_send()


def finish_kernel(nl, part_ref, c_ref, p_ref, shr_ref, inv_ref, out_ref):
    wide = p_ref[...].astype(F32)
    for l in range(nl):
        scaled = (shr_ref[:, l:l + 1] * wide).astype(BF16)
        fitted = jnp.dot(c_ref[...], scaled, preferred_element_type=F32)
        out_ref[l] = part_ref[l] - fitted * inv_ref[:, l:l + 1]


def local(n, nt, samples, traits, whitening, singular, lambdas):
    tall, k = samples.shape
    own_k = whitening.shape[1]
    wide = traits.shape[1]
    nl = lambdas.shape[0]
    bits = n.bit_length() - 1
    unit = ROWS << bits
    halves = 2 if wide % (2 * LANES) == 0 else 1
    cols = wide // halves
    blocks = max(own_k // unit, 1)
    rows = k // unit
    units = rows * halves
    late = ((units - 1) % WAVE + 1) // halves * unit
    wave_k = WAVE // halves * unit
    vmem = pl.BlockSpec(memory_space=pltpu.VMEM)
    partial, components, projected, shrink, inverse = pl.pallas_call(
        functools.partial(exchange_kernel, n, nt, nl, halves),
        out_shape=[
            jax.ShapeDtypeStruct((nl, tall, wide), F32),
            jax.ShapeDtypeStruct((tall, late), BF16),
            jax.ShapeDtypeStruct((late, wide), BF16),
            jax.ShapeDtypeStruct((late, LANES), F32),
            jax.ShapeDtypeStruct((tall, LANES), F32),
        ],
        in_specs=[pl.BlockSpec(memory_space=pl.ANY)] * 3 + [vmem, pl.BlockSpec(memory_space=pltpu.SMEM)],
        out_specs=[pl.BlockSpec(memory_space=pl.ANY)] + [vmem] * 4,
        scratch_shapes=[
            pltpu.VMEM(samples.shape, BF16),
            pltpu.VMEM(whitening.shape, BF16),
            pltpu.VMEM(traits.shape, BF16),
            pltpu.VMEM((units, unit, cols), F32),
            pltpu.VMEM((units, unit, cols), BF16),
            pltpu.VMEM((units, unit, cols), BF16),
            pltpu.VMEM((nt, tall, own_k), BF16),
            pltpu.VMEM((units, unit, cols), BF16),
            pltpu.VMEM((k, LANES), F32),
            pltpu.VMEM((nl, tall, wide), F32),
            pltpu.VMEM((tall, wave_k), BF16),
            pltpu.VMEM((wave_k, cols), BF16),
            pltpu.SemaphoreType.DMA((nl,)),
            pltpu.SemaphoreType.DMA,
            pltpu.SemaphoreType.DMA((blocks,)),
            pltpu.SemaphoreType.DMA,
            pltpu.SemaphoreType.DMA((units, bits)),
            pltpu.SemaphoreType.DMA((units, bits)),
            pltpu.SemaphoreType.DMA((units, bits)),
            pltpu.SemaphoreType.DMA((units, bits)),
            pltpu.SemaphoreType.DMA((nt - 1,)),
            pltpu.SemaphoreType.DMA((nt - 1,)),
        ],
        compiler_params=pltpu.CompilerParams(
            collective_id=0, has_side_effects=True, vmem_limit_bytes=56 * 2**20
        ),
        name="project_and_sum",
    )(samples, whitening, traits, singular.reshape(1, k), lambdas)
    tile = min(2 * LANES, wide)
    return pl.pallas_call(
        functools.partial(finish_kernel, nl),
        grid=(wide // tile,),
        out_shape=jax.ShapeDtypeStruct((nl, tall, wide), F32),
        in_specs=[
            pl.BlockSpec((nl, tall, tile), lambda i: (0, 0, i)),
            pl.BlockSpec((tall, late), lambda i: (0, 0)),
            pl.BlockSpec((late, tile), lambda i: (0, i)),
            pl.BlockSpec((late, LANES), lambda i: (0, 0)),
            pl.BlockSpec((tall, LANES), lambda i: (0, 0)),
        ],
        out_specs=pl.BlockSpec((nl, tall, tile), lambda i: (0, 0, i)),
        compiler_params=pltpu.CompilerParams(vmem_limit_bytes=60 * 2**20),
        name="finish",
    )(partial, components, projected, shrink, inverse)


def solution(mesh):
    n, nt = mesh.shape["samp"], mesh.shape["trait"]
    return jax.shard_map(
        functools.partial(local, n, nt),
        mesh=mesh,
        in_specs=(P("samp", None), P("samp", "trait"), P(None, "trait"), P(), P()),
        out_specs=P(None, "samp", "trait"),
        check_vma=False,
    )
```
